256 devices in a mesh: tile: 64 (over z, y, core), pair: 4 (over x).
Axes of the slice: x: 4, y: 4, z: 8, core: 2. Of those that a mesh axis runs over, the one named last changes fastest.
Arguments:
- slc: bfloat16 [128, 128, 2, 8192], P('tile'), may hold values from -64 to 64
- pairs: int32 [384, 2], replicated, may hold values from 0 to 127, as said below
- groups: int32 [384, 1], replicated, may hold values from 0 to 3; in each aligned block of 384 rows (0 to 383, 384 to 767, ...) at most 192 rows name the same one
- tile_source: int32 [128], replicated, may hold values from 0 to 127, each once
Outputs:
- rhs: float32 [128, 128, 2, 128], P('pair', 'tile')
- coherence: float32 [768, 128, 128], P('pair', 'tile')
The draws below stay inside these ranges and needn't reach their ends.
Inputs may be any that keep to these rules, and one draw needn't show every extreme that they name: `pairs`: every row holds two different epochs, the smaller first, and every epoch appears in some row. `groups`: at most 192 pairs belong to one group, and one group has exactly 192.
All inputs are finite; a program needn't handle non-finite values.
Results may differ from the reference program's by a relative error of at most 0.0003.
Values may be sent and summed in bfloat16 or wider, within the bound.
No kernel may reach another device: no remote copies, remote signals or barrier semaphores. Data moves between devices by JAX's collectives and lax.ppermute only.
A program may use at most 128 MiB of HBM per device.

```python
import math
import jax
import jax.numpy as jnp
import numpy as np
from jax import lax

AT = 16
TR = 512
E = 128
NT = 128
NPAIR = 384
PCAP = 192
N_PAIR = 4


def draw_pairs(key, part):
    first = jnp.arange(NPAIR, dtype=jnp.int32) % E
    gap = jax.random.randint(key, (NPAIR,), 1, E, dtype=jnp.int32)
    second = (first + gap) % E
    return jnp.stack([jnp.minimum(first, second), jnp.maximum(first, second)], axis=1)


def draw_slc(key, part):
    keys = jax.random.split(key, 7)
    shape = (NT, AT * TR)
    common_re = jax.random.normal(keys[0], shape, jnp.float32)
    common_im = jax.random.normal(keys[1], shape, jnp.float32)
    amplitude = jnp.exp(jax.random.uniform(keys[2], shape, jnp.float32, math.log(0.3), math.log(3.0)))
    fraction = jax.random.uniform(keys[3], shape, jnp.float32, 0.5, 0.95)
    phase = jax.random.uniform(keys[4], (E, NT, 1), jnp.float32, -math.pi, math.pi)
    noise_re = jax.random.normal(keys[5], (E,) + shape, jnp.float32)
    noise_im = jax.random.normal(keys[6], (E,) + shape, jnp.float32)
    cosine = jnp.cos(phase)
    sine = jnp.sin(phase)
    rest = jnp.sqrt(1.0 - fraction * fraction)
    sample_re = amplitude * (fraction * (common_re * cosine - common_im * sine) + rest * noise_re)
    sample_im = amplitude * (fraction * (common_re * sine + common_im * cosine) + rest * noise_im)
    return jnp.stack([sample_re, sample_im], axis=2).astype(jnp.bfloat16)


def routed_block(rng, own, number, rows, amount, top, most, lean):
    ranking = jax.random.permutation(rng, amount)
    heavy_load, usual = shares(amount, rows * top, most, lean, True), shares(amount, rows * top, most, lean, False)
    places = jnp.arange(amount)

    def named(tallies, turn):
        used = int((tallies > 0).sum())
        fixed = max(1, used // 4)
        moved = fixed + (places - fixed + turn * (used - fixed)) % max(1, amount - fixed)
        return jnp.zeros((amount,), jnp.int32).at[ranking[jnp.where(places < fixed, places, moved)]].set(jnp.asarray(tallies, jnp.int32))

    tallies = jnp.where(number % 4 == 0, named(heavy_load, number // 4), named(usual, number - number // 4 - 1))
    mixed = jax.random.permutation(jax.random.fold_in(own, 3), amount)
    donor, receiver = mixed[0:amount // 2 * 2:2], mixed[1:amount // 2 * 2:2]
    margin = jnp.minimum(tallies[donor] - 1, most - tallies[receiver]) // 2
    margin = jnp.where((donor == ranking[0]) | (receiver == ranking[0]) | (tallies[receiver] == 0), 0, jnp.maximum(margin, 0))
    moved = jax.random.randint(jax.random.fold_in(own, 4), (amount // 2,), 0, 1 << 20) % (margin + 1)
    tallies = tallies.at[donor].add(-moved).at[receiver].add(moved)
    items = jnp.searchsorted(jnp.cumsum(tallies), jnp.arange(rows * top), side="right").astype(jnp.int32)
    table = items.reshape(top, rows).T
    table = table[jax.random.permutation(jax.random.fold_in(own, 1), rows)]
    turn = jax.random.randint(jax.random.fold_in(own, 2), (rows, 1), 0, top)
    return jnp.take_along_axis(table, (jnp.arange(top)[None, :] + turn) % top, axis=1)


def shares(count, total, reach, slope, full):
    loads = [(1 << 20) // math.isqrt(rank ** slope) + 1 for rank in range(1, count + 1)]
    largest = reach if full else min(reach, max(-(-total // count), total * loads[0] // sum(loads)))
    least = 1 if total - largest >= count - 1 else 0
    holding, surplus = [largest] + [least] * (count - 1), total - largest - least * (count - 1)
    while surplus > 0:
        free = [i for i in range(1, count) if holding[i] < largest] or [i for i in range(1, count) if holding[i] < reach]
        pool, budget = sum([loads[i] for i in free]), surplus
        for i in free:
            more = min(reach - holding[i], max(1, budget * loads[i] // pool), surplus)
            holding[i] = holding[i] + more
            surplus = surplus - more
    return np.array(holding)


def setup_inputs(seed: int = 0) -> dict:
    seeds = jax.random.split(jax.random.key(seed), 5)
    slc = draw_slc(jax.random.fold_in(seeds[4], 71), 0)
    pairs = draw_pairs(jax.random.fold_in(seeds[4], 71), 0)
    groups_keys = jax.random.split(jax.random.fold_in(seeds[2], 1), NPAIR // NPAIR)
    groups_turns = jax.random.permutation(jax.random.fold_in(seeds[2], 3), NPAIR // NPAIR)
    groups = jax.vmap(lambda own, number: routed_block(jax.random.fold_in(seeds[2], 2), own, number, NPAIR, N_PAIR, 1, PCAP, 2))(groups_keys, groups_turns).reshape((NPAIR, 1))
    tile_source = jax.random.permutation(seeds[3], NT).astype(jnp.int32)
    return {"slc": slc, "pairs": pairs, "groups": groups, "tile_source": tile_source}


EPS = 1e-06

def box_mean(values):
    lead = values.shape[:-1]
    grid = values.astype(jnp.float32).reshape(lead + (AT // 4, 4, TR // 16, 16))
    return (lax.optimization_barrier(jnp.sum(grid, axis=(-3, -1))) * (1.0 / 64.0)).reshape(lead + (AT * TR // 64,))

def tile_terms(data, refs, secs):
    d_re = data[:, 0].astype(jnp.float32)
    d_im = data[:, 1].astype(jnp.float32)
    a_re = jnp.take(d_re, refs, axis=0)
    a_im = jnp.take(d_im, refs, axis=0)
    b_re = jnp.take(d_re, secs, axis=0)
    b_im = jnp.take(d_im, secs, axis=0)
    cross_re = a_re * b_re + a_im * b_im
    cross_im = a_im * b_re - a_re * b_im
    power = d_re * d_re + d_im * d_im
    inter_re = box_mean(cross_re)
    inter_im = box_mean(cross_im)
    level = box_mean(power)
    scale = lax.rsqrt(jnp.take(level, refs, axis=0) + EPS) * lax.rsqrt(jnp.take(level, secs, axis=0) + EPS)
    gamma_re = inter_re * scale
    gamma_im = inter_im * scale
    weight = gamma_re * gamma_re + gamma_im * gamma_im
    weighted = jnp.stack([weight * gamma_re, weight * gamma_im], axis=1)
    epochs = jnp.arange(E, dtype=jnp.int32)[:, None]
    incidence = (epochs == secs[None, :]).astype(jnp.float32) - (epochs == refs[None, :]).astype(jnp.float32)
    rhs = jnp.dot(incidence, weighted.reshape(NPAIR, -1), precision=lax.Precision.HIGHEST, preferred_element_type=jnp.float32)
    return (weight, rhs.reshape(E, 2, AT * TR // 64))

def reference(slc, pairs, groups, tile_source):
    refs = pairs[:, 0].astype(jnp.int32)
    secs = pairs[:, 1].astype(jnp.int32)

    def one_tile(source):
        data = jnp.take(slc, source, axis=1)
        return tile_terms(data, refs, secs)
    weight_all, rhs_all = lax.map(one_tile, tile_source.astype(jnp.int32))
    rhs = jnp.transpose(rhs_all, (1, 0, 2, 3))
    group_ids = jnp.arange(N_PAIR, dtype=jnp.int32)[:, None]
    mine = groups[:, 0].astype(jnp.int32)[None, :] == group_ids
    rank = jnp.cumsum(mine.astype(jnp.int32), axis=1) - 1
    slots = jnp.arange(PCAP, dtype=jnp.int32)[None, :, None]
    hit = mine[:, None, :] & (rank[:, None, :] == slots)
    pair_ids = jnp.arange(NPAIR, dtype=jnp.int32)[None, None, :]
    slot_pair = lax.optimization_barrier(jnp.sum(jnp.where(hit, pair_ids, 0), axis=2)).astype(jnp.int32)
    live = jnp.any(hit, axis=2).astype(jnp.float32)
    chosen = jnp.take(weight_all, slot_pair.reshape(-1), axis=1) * live.reshape(-1)[None, :, None]
    coherence = jnp.transpose(chosen, (1, 0, 2))
    return (rhs, coherence)
```

```python
import functools

import jax
import jax.numpy as jnp
from jax import lax
from jax.experimental import pallas as pl
from jax.experimental.pallas import tpu as pltpu
from jax.sharding import PartitionSpec as P

EPS = 1e-06
LOOK_PIXELS = 64
LANES = 128
BATCH = 8


def split_dot(ones, x):
    high = x.astype(jnp.bfloat16)
    rest = x - high.astype(jnp.float32)
    middle = rest.astype(jnp.bfloat16)
    low = (rest - middle.astype(jnp.float32)).astype(jnp.bfloat16)
    width = x.shape[1]
    out = jnp.dot(ones, jnp.concatenate([high, middle, low], axis=1), preferred_element_type=jnp.float32)
    return out[:, :width] + out[:, width : 2 * width] + out[:, 2 * width :]


def dot_split(x, ones):
    high = x.astype(jnp.bfloat16)
    rest = x - high.astype(jnp.float32)
    middle = rest.astype(jnp.bfloat16)
    low = (rest - middle.astype(jnp.float32)).astype(jnp.bfloat16)
    rows = x.shape[0]
    out = jnp.dot(jnp.concatenate([high, middle, low], axis=0), ones, preferred_element_type=jnp.float32)
    return out[:rows] + out[rows : 2 * rows] + out[2 * rows :]


def order_kernel(source_ref, slc_ref, out_ref, sem):
    n_dev, _, tiles_dev, _, part = out_ref.shape
    start = pl.multiple_of(lax.axis_index("pair") * part, part)

    @pl.loop(0, n_dev)
    def _(d):
        for k in range(tiles_dev):
            src = source_ref[d * tiles_dev + k]
            pltpu.make_async_copy(
                slc_ref.at[:, src, :, pl.ds(start, part)], out_ref.at[d, :, k], sem
            ).start()

    pltpu.make_async_copy(out_ref, out_ref, sem).wait()


def lane_bit(bit):
    return (lax.broadcasted_iota(jnp.int32, (8, LANES), 1) & bit) == 0


def terms_kernel(pairs_sm, data_ref, pairs_ref, groups_ref, out_ref, wide, norm, gamma):
    n_epochs = data_ref.shape[0]
    n_pairs = pairs_ref.shape[1]
    step = wide.shape[0]
    sub = lax.broadcasted_iota(jnp.int32, (8, LANES), 0)
    lane = lax.broadcasted_iota(jnp.int32, (8, LANES), 1)
    first = sub < 4
    rows_i = lax.broadcasted_iota(jnp.int32, (LANES, LANES), 0)
    cols_i = lax.broadcasted_iota(jnp.int32, (LANES, LANES), 1)
    same_look = (rows_i // 16 == cols_i // 16).astype(jnp.bfloat16)

    @pl.loop(0, n_epochs // step)
    def _(block):
        at = pl.ds(block * step, step)
        wide[...] = data_ref[at].astype(jnp.float32)
        re = wide[:, :, pl.ds(0, 16, stride=2), :]
        im = wide[:, :, pl.ds(1, 16, stride=2), :]
        power = re * re + im * im
        lines = power[:, :, 0:8] + power[:, :, 8:16]
        lines = lines + pltpu.roll(lines, 4, 2)
        level = dot_split(lines.reshape(step * 2 * 8, LANES), same_look).reshape(step, 2, 8, LANES)
        inv = lax.rsqrt(level * (1.0 / LOOK_PIXELS) + EPS) * 0.125
        inv = jnp.concatenate([inv, inv], axis=2)
        norm[at, 0] = re * inv
        norm[at, 1] = im * inv

    @pl.loop(0, n_pairs // BATCH)
    def _(batch):
        def one(j):
            q = batch * BATCH + j
            r = pairs_sm[0, q]
            t = pairs_sm[1, q]
            a_re, a_im = norm[r, 0], norm[r, 1]
            b_re, b_im = norm[t, 0], norm[t, 1]
            parts = []
            for cross in (a_re * b_re + a_im * b_im, a_im * b_re - a_re * b_im):
                s0 = cross[0, 0:8] + cross[0, 8:16]
                s1 = cross[1, 0:8] + cross[1, 8:16]
                parts.append(jnp.where(first, s0, s1) + pltpu.roll(jnp.where(first, s1, s0), 4, 0))
            return merge(parts[0], parts[1], 8)

        def merge(a, b, k):
            return jnp.where(
                (lane & k) == 0, a + pltpu.roll(a, LANES - k, 1), b + pltpu.roll(b, k, 1)
            )

        def tree(js, k):
            if len(js) == 1:
                return one(js[0])
            return merge(tree([j for j in js if not j & k], k // 2), tree([j for j in js if j & k], k // 2), k)

        z = tree(list(range(BATCH)), 4)
        for k in (4, 2, 1):
            up = pltpu.roll(pltpu.roll(z, k, 1), 8 - k, 0)
            down = pltpu.roll(pltpu.roll(z, LANES - k, 1), k, 0)
            low_row, low_lane = (sub & k) == 0, (lane & k) == 0
            z = jnp.where(low_row == low_lane, z, jnp.where(low_row, up, down))
        gamma[pl.ds(pl.multiple_of(batch * BATCH, BATCH), BATCH), :] = z

    z = gamma[...]
    comp0 = (lax.broadcasted_iota(jnp.int32, z.shape, 1) & 8) == 0
    square = z * z
    weight = square + jnp.where(comp0, pltpu.roll(square, LANES - 8, 1), pltpu.roll(square, 8, 1))
    refs, secs, groups = pairs_ref[0:1, :], pairs_ref[1:2, :], groups_ref[0:1, :]
    epochs = lax.broadcasted_iota(jnp.int32, (n_epochs, n_pairs), 0)
    incidence = (epochs == secs).astype(jnp.float32) - (epochs == refs).astype(jnp.float32)
    rhs = split_dot(incidence.astype(jnp.bfloat16), weight * z)

    n_groups = out_ref.shape[0]
    mine = (lax.broadcasted_iota(jnp.int32, (8, n_pairs), 0) == groups).astype(jnp.float32)
    before = (
        lax.broadcasted_iota(jnp.int32, (n_pairs, n_pairs), 0)
        < lax.broadcasted_iota(jnp.int32, (n_pairs, n_pairs), 1)
    )
    ranks = jnp.dot(
        mine.astype(jnp.bfloat16), before.astype(jnp.bfloat16), preferred_element_type=jnp.float32
    )
    rank = jnp.sum(mine * ranks, axis=0, keepdims=True).astype(jnp.int32)
    half = n_pairs // 4
    slot = jnp.where(rank < half, groups * half + rank, n_pairs + groups * half + rank - half)
    hit = (lax.broadcasted_iota(jnp.int32, (2 * n_pairs, n_pairs), 0) == slot).astype(jnp.bfloat16)
    chosen = split_dot(hit, weight)
    chosen = jnp.where(comp0, chosen[:n_pairs], chosen[n_pairs:])
    e_out = n_epochs // n_groups
    for g in range(n_groups):
        out_ref[g, 0:half, :] = chosen[g * half : (g + 1) * half]
        out_ref[g, half : half + e_out, :] = rhs[g * e_out : (g + 1) * e_out]


def place_kernel(parts_ref, rhs_ref, coherence_ref):
    n_parts, rows, _ = parts_ref.shape
    half = coherence_ref.shape[0] // 2
    i = lax.broadcasted_iota(jnp.int32, (LANES, LANES), 0)
    j = lax.broadcasted_iota(jnp.int32, (LANES, LANES), 1)
    total = [[None, None], [None, None]]
    for q in range(n_parts):
        ones = []
        for comp in range(2):
            for slot in range(2):
                look = q * 32 + (i & 3) * 8 + i // 16
                ones.append(
                    ((j == look) & (((i // 8) & 1) == comp) & (((i // 4) & 1) == slot)).astype(jnp.bfloat16)
                )
        out = dot_split(parts_ref[q], jnp.concatenate(ones, axis=1))
        for comp in range(2):
            for slot in range(2):
                k = comp * 2 + slot
                piece = out[:, k * LANES : (k + 1) * LANES]
                total[comp][slot] = piece if q == 0 else total[comp][slot] + piece
    for comp in range(2):
        for slot in range(2):
            coherence_ref[pl.ds(comp * half, half), slot, :] = total[comp][slot][:half]
            rhs_ref[:, slot, comp, :] = total[comp][slot][half:]


def local(slc, pairs, groups, tile_source):
    n_tile, n_pair = lax.axis_size("tile"), lax.axis_size("pair")
    e_dev, n_tiles, _, pixels = slc.shape
    tiles_dev = n_tiles // n_tile
    part = pixels // n_pair
    n_pairs = pairs.shape[0]
    n_epochs = e_dev * n_tile
    any_space = pl.BlockSpec(memory_space=pl.ANY)
    scalars = pl.BlockSpec(memory_space=pltpu.SMEM)
    vector = pl.BlockSpec(memory_space=pltpu.VMEM)
    ordered = pl.pallas_call(
        order_kernel,
        out_shape=jax.ShapeDtypeStruct((n_tile, e_dev, tiles_dev, 2, part), slc.dtype),
        in_specs=[scalars, any_space],
        out_specs=any_space,
        scratch_shapes=[pltpu.SemaphoreType.DMA],
        name="order",
    )(tile_source, slc)
    data = lax.all_to_all(ordered, "tile", split_axis=0, concat_axis=0, tiled=True)
    data = data.reshape(n_epochs, tiles_dev, 2, part // LANES, LANES)
    data = jnp.swapaxes(data, 2, 3).reshape(n_epochs, tiles_dev, 2 * part // LANES, LANES)
    pairs_t = pairs.T
    rows = n_pairs // 4 + n_epochs // n_pair
    parts = pl.pallas_call(
        terms_kernel,
        out_shape=jax.ShapeDtypeStruct((n_pair, rows, LANES), jnp.float32),
        in_specs=[scalars, vector, vector, vector],
        out_specs=vector,
        scratch_shapes=[
            pltpu.VMEM((8, tiles_dev, 32, LANES), jnp.float32),
            pltpu.VMEM((n_epochs, 2, tiles_dev, 16, LANES), jnp.float32),
            pltpu.VMEM((n_pairs, LANES), jnp.float32),
        ],
        compiler_params=pltpu.CompilerParams(vmem_limit_bytes=40 * 1024 * 1024),
        name="terms",
    )(pairs_t, data, pairs_t, groups.reshape(1, n_pairs))
    parts = lax.all_to_all(parts, "pair", split_axis=0, concat_axis=0, tiled=True)
    return pl.pallas_call(
        place_kernel,
        out_shape=(
            jax.ShapeDtypeStruct((n_epochs // n_pair, tiles_dev, 2, LANES), jnp.float32),
            jax.ShapeDtypeStruct((n_pairs // 2, tiles_dev, LANES), jnp.float32),
        ),
        in_specs=[vector],
        out_specs=(vector, vector),
        name="place",
    )(parts)


def solution(mesh):
    placed = (P("tile", None, None, None), P(), P(), P())
    return jax.shard_map(
        local,
        mesh=mesh,
        in_specs=placed,
        out_specs=(P("pair", "tile", None, None), P("pair", "tile", None)),
        check_vma=False,
    )
```

```python
import functools

import jax
import jax.numpy as jnp
from jax import lax
from jax.experimental import pallas as pl
from jax.experimental.pallas import tpu as pltpu
from jax.sharding import PartitionSpec as P

EPS = 1e-06
LOOK_PIXELS = 64
LANES = 128
BATCH = 8


def split_dot(ones, x):
    high = x.astype(jnp.bfloat16)
    rest = x - high.astype(jnp.float32)
    middle = rest.astype(jnp.bfloat16)
    low = (rest - middle.astype(jnp.float32)).astype(jnp.bfloat16)
    width = x.shape[1]
    out = jnp.dot(ones, jnp.concatenate([high, middle, low], axis=1), preferred_element_type=jnp.float32)
    return out[:, :width] + out[:, width : 2 * width] + out[:, 2 * width :]


def dot_split(x, ones):
    high = x.astype(jnp.bfloat16)
    rest = x - high.astype(jnp.float32)
    middle = rest.astype(jnp.bfloat16)
    low = (rest - middle.astype(jnp.float32)).astype(jnp.bfloat16)
    rows = x.shape[0]
    out = jnp.dot(jnp.concatenate([high, middle, low], axis=0), ones, preferred_element_type=jnp.float32)
    return out[:rows] + out[rows : 2 * rows] + out[2 * rows :]


def order_kernel(source_ref, slc_ref, out_ref, sem):
    n_dev, _, tiles_dev, _, part = out_ref.shape
    start = pl.multiple_of(lax.axis_index("pair") * part, part)

    @pl.loop(0, n_dev)
    def _(d):
        for k in range(tiles_dev):
            src = source_ref[d * tiles_dev + k]
            pltpu.make_async_copy(
                slc_ref.at[:, src, :, pl.ds(start, part)], out_ref.at[d, :, k], sem
            ).start()

    pltpu.make_async_copy(out_ref, out_ref, sem).wait()


def lane_bit(bit):
    return (lax.broadcasted_iota(jnp.int32, (8, LANES), 1) & bit) == 0


def terms_kernel(pairs_sm, data_ref, pairs_ref, groups_ref, out_ref, wide, norm, gamma):
    n_epochs = data_ref.shape[0]
    n_pairs = pairs_ref.shape[1]
    step = wide.shape[0]
    sub = lax.broadcasted_iota(jnp.int32, (8, LANES), 0)
    lane = lax.broadcasted_iota(jnp.int32, (8, LANES), 1)
    first = sub < 4
    rows_i = lax.broadcasted_iota(jnp.int32, (LANES, LANES), 0)
    cols_i = lax.broadcasted_iota(jnp.int32, (LANES, LANES), 1)
    same_look = (rows_i // 16 == cols_i // 16).astype(jnp.bfloat16)

    @pl.loop(0, n_epochs // step, unroll=2)
    def _(block):
        at = pl.ds(block * step, step)
        wide[...] = data_ref[at].astype(jnp.float32)
        re = wide[:, :, pl.ds(0, 16, stride=2), :]
        im = wide[:, :, pl.ds(1, 16, stride=2), :]
        power = re * re + im * im
        lines = power[:, :, 0:8] + power[:, :, 8:16]
        lines = lines + pltpu.roll(lines, 4, 2)
        level = dot_split(lines.reshape(step * 2 * 8, LANES), same_look).reshape(step, 2, 8, LANES)
        inv = lax.rsqrt(level * (1.0 / LOOK_PIXELS) + EPS) * 0.125
        inv = jnp.concatenate([inv, inv], axis=2)
        norm[at, 0] = re * inv
        norm[at, 1] = im * inv

    @pl.loop(0, n_pairs // BATCH, unroll=8)
    def _(batch):
        def one(j):
            q = batch * BATCH + j
            r = pairs_sm[0, q]
            t = pairs_sm[1, q]
            a_re, a_im = norm[r, 0], norm[r, 1]
            b_re, b_im = norm[t, 0], norm[t, 1]
            parts = []
            for cross in (a_re * b_re + a_im * b_im, a_im * b_re - a_re * b_im):
                s0 = cross[0, 0:8] + cross[0, 8:16]
                s1 = cross[1, 0:8] + cross[1, 8:16]
                parts.append(jnp.where(first, s0, s1) + pltpu.roll(jnp.where(first, s1, s0), 4, 0))
            return merge(parts[0], parts[1], 8)

        def merge(a, b, k):
            return jnp.where(
                (lane & k) == 0, a + pltpu.roll(a, LANES - k, 1), b + pltpu.roll(b, k, 1)
            )

        def tree(js, k):
            if len(js) == 1:
                return one(js[0])
            return merge(tree([j for j in js if not j & k], k // 2), tree([j for j in js if j & k], k // 2), k)

        z = tree(list(range(BATCH)), 4)
        for k in (4, 2, 1):
            up = pltpu.roll(pltpu.roll(z, k, 1), 8 - k, 0)
            down = pltpu.roll(pltpu.roll(z, LANES - k, 1), k, 0)
            low_row, low_lane = (sub & k) == 0, (lane & k) == 0
            z = jnp.where(low_row == low_lane, z, jnp.where(low_row, up, down))
        gamma[pl.ds(pl.multiple_of(batch * BATCH, BATCH), BATCH), :] = z

    z = gamma[...]
    comp0 = (lax.broadcasted_iota(jnp.int32, z.shape, 1) & 8) == 0
    square = z * z
    weight = square + jnp.where(comp0, pltpu.roll(square, LANES - 8, 1), pltpu.roll(square, 8, 1))
    refs, secs, groups = pairs_ref[0:1, :], pairs_ref[1:2, :], groups_ref[0:1, :]
    epochs = lax.broadcasted_iota(jnp.int32, (n_epochs, n_pairs), 0)
    incidence = (epochs == secs).astype(jnp.float32) - (epochs == refs).astype(jnp.float32)
    rhs = split_dot(incidence.astype(jnp.bfloat16), weight * z)

    n_groups = out_ref.shape[0]
    mine = (lax.broadcasted_iota(jnp.int32, (8, n_pairs), 0) == groups).astype(jnp.float32)
    before = (
        lax.broadcasted_iota(jnp.int32, (n_pairs, n_pairs), 0)
        < lax.broadcasted_iota(jnp.int32, (n_pairs, n_pairs), 1)
    )
    ranks = jnp.dot(
        mine.astype(jnp.bfloat16), before.astype(jnp.bfloat16), preferred_element_type=jnp.float32
    )
    rank = jnp.sum(mine * ranks, axis=0, keepdims=True).astype(jnp.int32)
    half = n_pairs // 4
    slot = jnp.where(rank < half, groups * half + rank, n_pairs + groups * half + rank - half)
    hit = (lax.broadcasted_iota(jnp.int32, (2 * n_pairs, n_pairs), 0) == slot).astype(jnp.bfloat16)
    chosen = split_dot(hit, weight)
    chosen = jnp.where(comp0, chosen[:n_pairs], chosen[n_pairs:])
    e_out = n_epochs // n_groups
    for g in range(n_groups):
        out_ref[g, 0:half, :] = chosen[g * half : (g + 1) * half]
        out_ref[g, half : half + e_out, :] = rhs[g * e_out : (g + 1) * e_out]


def place_kernel(parts_ref, rhs_ref, coherence_ref):
    n_parts, rows, _ = parts_ref.shape
    half = coherence_ref.shape[0] // 2
    i = lax.broadcasted_iota(jnp.int32, (LANES, LANES), 0)
    j = lax.broadcasted_iota(jnp.int32, (LANES, LANES), 1)
    total = [[None, None], [None, None]]
    for q in range(n_parts):
        ones = []
        for comp in range(2):
            for slot in range(2):
                look = q * 32 + (i & 3) * 8 + i // 16
                ones.append(
                    ((j == look) & (((i // 8) & 1) == comp) & (((i // 4) & 1) == slot)).astype(jnp.bfloat16)
                )
        out = dot_split(parts_ref[q], jnp.concatenate(ones, axis=1))
        for comp in range(2):
            for slot in range(2):
                k = comp * 2 + slot
                piece = out[:, k * LANES : (k + 1) * LANES]
                total[comp][slot] = piece if q == 0 else total[comp][slot] + piece
    for comp in range(2):
        for slot in range(2):
            coherence_ref[pl.ds(comp * half, half), slot, :] = total[comp][slot][:half]
            rhs_ref[:, slot, comp, :] = total[comp][slot][half:]


def local(slc, pairs, groups, tile_source):
    n_tile, n_pair = lax.axis_size("tile"), lax.axis_size("pair")
    e_dev, n_tiles, _, pixels = slc.shape
    tiles_dev = n_tiles // n_tile
    part = pixels // n_pair
    n_pairs = pairs.shape[0]
    n_epochs = e_dev * n_tile
    any_space = pl.BlockSpec(memory_space=pl.ANY)
    scalars = pl.BlockSpec(memory_space=pltpu.SMEM)
    vector = pl.BlockSpec(memory_space=pltpu.VMEM)
    ordered = pl.pallas_call(
        order_kernel,
        out_shape=jax.ShapeDtypeStruct((n_tile, e_dev, tiles_dev, 2, part), slc.dtype),
        in_specs=[scalars, any_space],
        out_specs=vector,
        scratch_shapes=[pltpu.SemaphoreType.DMA],
        name="order",
    )(tile_source, slc)
    data = lax.all_to_all(ordered, "tile", split_axis=0, concat_axis=0, tiled=True)
    data = data.reshape(n_epochs, tiles_dev, 2, part // LANES, LANES)
    data = jnp.swapaxes(data, 2, 3).reshape(n_epochs, tiles_dev, 2 * part // LANES, LANES)
    pairs_t = pairs.T
    rows = n_pairs // 4 + n_epochs // n_pair
    parts = pl.pallas_call(
        terms_kernel,
        out_shape=jax.ShapeDtypeStruct((n_pair, rows, LANES), jnp.float32),
        in_specs=[scalars, vector, vector, vector],
        out_specs=vector,
        scratch_shapes=[
            pltpu.VMEM((8, tiles_dev, 32, LANES), jnp.float32),
            pltpu.VMEM((n_epochs, 2, tiles_dev, 16, LANES), jnp.float32),
            pltpu.VMEM((n_pairs, LANES), jnp.float32),
        ],
        compiler_params=pltpu.CompilerParams(vmem_limit_bytes=40 * 1024 * 1024),
        name="terms",
    )(pairs_t, data, pairs_t, groups.reshape(1, n_pairs))
    parts = lax.all_to_all(parts, "pair", split_axis=0, concat_axis=0, tiled=True)
    return pl.pallas_call(
        place_kernel,
        out_shape=(
            jax.ShapeDtypeStruct((n_epochs // n_pair, tiles_dev, 2, LANES), jnp.float32),
            jax.ShapeDtypeStruct((n_pairs // 2, tiles_dev, LANES), jnp.float32),
        ),
        in_specs=[vector],
        out_specs=(vector, vector),
        name="place",
    )(parts)


def solution(mesh):
    placed = (P("tile", None, None, None), P(), P(), P())
    return jax.shard_map(
        local,
        mesh=mesh,
        in_specs=placed,
        out_specs=(P("pair", "tile", None, None), P("pair", "tile", None)),
        check_vma=False,
    )
```

```python
import functools

import jax
import jax.numpy as jnp
from jax import lax
from jax.experimental import pallas as pl
from jax.experimental.pallas import tpu as pltpu
from jax.sharding import PartitionSpec as P

EPS = 1e-06
LOOK_PIXELS = 64
LANES = 128
BATCH = 8


def split_dot(ones, x):
    high = x.astype(jnp.bfloat16)
    rest = x - high.astype(jnp.float32)
    middle = rest.astype(jnp.bfloat16)
    low = (rest - middle.astype(jnp.float32)).astype(jnp.bfloat16)
    width = x.shape[1]
    out = jnp.dot(ones, jnp.concatenate([high, middle, low], axis=1), preferred_element_type=jnp.float32)
    return out[:, :width] + out[:, width : 2 * width] + out[:, 2 * width :]


def dot_split(x, ones):
    high = x.astype(jnp.bfloat16)
    rest = x - high.astype(jnp.float32)
    middle = rest.astype(jnp.bfloat16)
    low = (rest - middle.astype(jnp.float32)).astype(jnp.bfloat16)
    rows = x.shape[0]
    out = jnp.dot(jnp.concatenate([high, middle, low], axis=0), ones, preferred_element_type=jnp.float32)
    return out[:rows] + out[rows : 2 * rows] + out[2 * rows :]


def order_kernel(source_ref, slc_ref, groups_ref, held, slot_ref, in_sem):
    n_dev, _, tiles_dev, _, part = held.shape
    n_chunks = in_sem.shape[0]
    chunk = n_dev // n_chunks
    start = pl.multiple_of(lax.axis_index("pair") * part, part)

    for c in range(n_chunks):

        @pl.loop(c * chunk, (c + 1) * chunk, unroll=4)
        def _(d):
            for k in range(tiles_dev):
                src = source_ref[d * tiles_dev + k]
                pltpu.make_async_copy(
                    slc_ref.at[:, src, :, pl.ds(start, part)], held.at[d, :, k], in_sem.at[c]
                ).start()

    groups = groups_ref[0:1, :]
    n_pairs = groups.shape[1]
    mine = (lax.broadcasted_iota(jnp.int32, (8, n_pairs), 0) == groups).astype(jnp.float32)
    before = (
        lax.broadcasted_iota(jnp.int32, (n_pairs, n_pairs), 0)
        < lax.broadcasted_iota(jnp.int32, (n_pairs, n_pairs), 1)
    )
    ranks = jnp.dot(
        mine.astype(jnp.bfloat16), before.astype(jnp.bfloat16), preferred_element_type=jnp.float32
    )
    rank = jnp.sum(mine * ranks, axis=0, keepdims=True).astype(jnp.int32)
    half = n_pairs // 4
    slot = jnp.where(rank < half, groups * half + rank, n_pairs + groups * half + rank - half)
    slot_ref[...] = jnp.broadcast_to(slot, slot_ref.shape)

    for c in range(n_chunks):
        at = pl.ds(c * chunk, chunk)
        pltpu.make_async_copy(held.at[at], held.at[at], in_sem.at[c]).wait()


def terms_kernel(pairs_sm, data_ref, pairs_ref, slot_ref, *refs):
    out_refs, (wide, norm, gamma, chosen_ref, rhs_ref) = refs[:-5], refs[-5:]
    n_epochs = data_ref.shape[0]
    n_pairs = pairs_ref.shape[1]
    step = wide.shape[0]
    sub = lax.broadcasted_iota(jnp.int32, (8, LANES), 0)
    lane = lax.broadcasted_iota(jnp.int32, (8, LANES), 1)
    first = sub < 4
    rows_i = lax.broadcasted_iota(jnp.int32, (LANES, LANES), 0)
    cols_i = lax.broadcasted_iota(jnp.int32, (LANES, LANES), 1)
    same_look = (rows_i // 16 == cols_i // 16).astype(jnp.bfloat16)

    @pl.loop(0, n_epochs // step, unroll=4)
    def _(block):
        at = pl.ds(block * step, step)
        wide[...] = data_ref[at].astype(jnp.float32)
        re = wide[:, :, pl.ds(0, 16, stride=2), :]
        im = wide[:, :, pl.ds(1, 16, stride=2), :]
        power = re * re + im * im
        lines = power[:, :, 0:8] + power[:, :, 8:16]
        lines = lines + pltpu.roll(lines, 4, 2)
        level = dot_split(lines.reshape(step * 2 * 8, LANES), same_look).reshape(step, 2, 8, LANES)
        inv = lax.rsqrt(level * (1.0 / LOOK_PIXELS) + EPS) * 0.125
        inv = jnp.concatenate([inv, inv], axis=2)
        norm[at, 0] = re * inv
        norm[at, 1] = im * inv

    @pl.loop(0, n_pairs // BATCH, unroll=8)
    def _(batch):
        def one(j):
            q = batch * BATCH + j
            r = pairs_sm[0, q]
            t = pairs_sm[1, q]
            a_re, a_im = norm[r, 0], norm[r, 1]
            b_re, b_im = norm[t, 0], norm[t, 1]
            parts = []
            for cross in (a_re * b_re + a_im * b_im, a_im * b_re - a_re * b_im):
                s0 = cross[0, 0:8] + cross[0, 8:16]
                s1 = cross[1, 0:8] + cross[1, 8:16]
                parts.append(jnp.where(first, s0, s1) + pltpu.roll(jnp.where(first, s1, s0), 4, 0))
            return merge(parts[0], parts[1], 8)

        def merge(a, b, k):
            return jnp.where(
                (lane & k) == 0, a + pltpu.roll(a, LANES - k, 1), b + pltpu.roll(b, k, 1)
            )

        def tree(js, k):
            if len(js) == 1:
                return one(js[0])
            return merge(tree([j for j in js if not j & k], k // 2), tree([j for j in js if j & k], k // 2), k)

        z = tree(list(range(BATCH)), 4)
        gamma[batch] = z

    z = gamma[...]
    sub = lax.broadcasted_iota(jnp.int32, z.shape, 1)
    lane = lax.broadcasted_iota(jnp.int32, z.shape, 2)
    for k in (4, 2, 1):
        up = pltpu.roll(pltpu.roll(z, k, 2), 8 - k, 1)
        down = pltpu.roll(pltpu.roll(z, LANES - k, 2), k, 1)
        low_row, low_lane = (sub & k) == 0, (lane & k) == 0
        z = jnp.where(low_row == low_lane, z, jnp.where(low_row, up, down))
    z = z.reshape(n_pairs, LANES)
    comp0 = (lax.broadcasted_iota(jnp.int32, z.shape, 1) & 8) == 0
    square = z * z
    weight = square + jnp.where(comp0, pltpu.roll(square, LANES - 8, 1), pltpu.roll(square, 8, 1))
    refs, secs = pairs_ref[0:1, :], pairs_ref[1:2, :]
    epochs = lax.broadcasted_iota(jnp.int32, (n_epochs, n_pairs), 0)
    incidence = (epochs == secs).astype(jnp.float32) - (epochs == refs).astype(jnp.float32)
    rhs_ref[...] = split_dot(incidence.astype(jnp.bfloat16), weight * z)
    slot = slot_ref[0:1, :]
    hit = (lax.broadcasted_iota(jnp.int32, (2 * n_pairs, n_pairs), 0) == slot).astype(jnp.bfloat16)
    chosen = split_dot(hit, weight)
    chosen_ref[...] = jnp.where(comp0, chosen[:n_pairs], chosen[n_pairs:])
    n_members = len(out_refs)
    half, e_out = n_pairs // n_members, n_epochs // n_members
    me = lax.axis_index("pair")
    for k, out_ref in enumerate(out_refs):
        to = lax.rem(me + k, n_members)
        out_ref[0:half, :] = chosen_ref[pl.ds(pl.multiple_of(to * half, half), half), :]
        out_ref[half : half + e_out, :] = rhs_ref[pl.ds(pl.multiple_of(to * e_out, e_out), e_out), :]


def place_kernel(*refs):
    part_refs, (rhs_ref, coherence_ref) = refs[:-2], refs[-2:]
    n_members = len(part_refs)
    rows = part_refs[0].shape[0]
    half = coherence_ref.shape[0] // 2
    width = LANES // n_members
    me = lax.axis_index("pair")
    i = lax.broadcasted_iota(jnp.int32, (LANES, LANES), 0)
    j = lax.broadcasted_iota(jnp.int32, (LANES, LANES), 1)
    ones = (j == (i % 16) * 8 + i // 16).astype(jnp.bfloat16)
    parts = dot_split(jnp.concatenate([r[...] for r in part_refs], axis=0), ones)
    owner = lax.broadcasted_iota(jnp.int32, (rows, LANES), 1) // width
    total = [None] * 4
    for k in range(n_members):
        member = lax.rem(me + n_members - k, n_members)
        own = owner == member
        base = pltpu.roll(parts[k * rows : (k + 1) * rows], member * width, 1)
        for g in range(4):
            piece = base if g == 0 else pltpu.roll(base, LANES - g * width, 1)
            total[g] = piece if k == 0 else jnp.where(own, piece, total[g])
    for comp in range(2):
        for slot in range(2):
            coherence_ref[pl.ds(comp * half, half), slot, :] = total[comp * 2 + slot][:half]
            rhs_ref[:, slot, comp, :] = total[comp * 2 + slot][half:]


def local(slc, pairs, groups, tile_source):
    n_tile, n_pair = lax.axis_size("tile"), lax.axis_size("pair")
    e_dev, n_tiles, _, pixels = slc.shape
    tiles_dev = n_tiles // n_tile
    part = pixels // n_pair
    n_pairs = pairs.shape[0]
    n_epochs = e_dev * n_tile
    in_hbm = pl.BlockSpec(memory_space=pltpu.HBM)
    scalars = pl.BlockSpec(memory_space=pltpu.SMEM)
    vector = pl.BlockSpec(memory_space=pltpu.VMEM)
    pairs_t, groups_t = pairs.T, groups.reshape(1, n_pairs)
    out_shape = (n_tile, e_dev, tiles_dev, 2, part)
    chunks = 4
    ordered, slots = pl.pallas_call(
        order_kernel,
        out_shape=(
            jax.ShapeDtypeStruct(out_shape, slc.dtype),
            jax.ShapeDtypeStruct((8, n_pairs), jnp.int32),
        ),
        in_specs=[scalars, in_hbm, vector],
        out_specs=(vector, vector),
        scratch_shapes=[
            pltpu.SemaphoreType.DMA((chunks,)),
        ],
        compiler_params=pltpu.CompilerParams(vmem_limit_bytes=8 * 1024 * 1024),
        name="order",
    )(tile_source, slc, groups_t)
    data = lax.all_to_all(ordered, "tile", split_axis=0, concat_axis=0, tiled=True)
    data = data.reshape(n_epochs, tiles_dev, 2, part // LANES, LANES)
    data = jnp.swapaxes(data, 2, 3).reshape(n_epochs, tiles_dev, 2 * part // LANES, LANES)
    rows = n_pairs // 4 + n_epochs // n_pair
    parts = pl.pallas_call(
        terms_kernel,
        out_shape=[jax.ShapeDtypeStruct((rows, LANES), jnp.float32)] * n_pair,
        in_specs=[scalars, vector, vector, vector],
        out_specs=[vector] * n_pair,
        scratch_shapes=[
            pltpu.VMEM((8, tiles_dev, 32, LANES), jnp.float32),
            pltpu.VMEM((n_epochs, 2, tiles_dev, 16, LANES), jnp.float32),
            pltpu.VMEM((n_pairs // BATCH, BATCH, LANES), jnp.float32),
            pltpu.VMEM((n_pairs, LANES), jnp.float32),
            pltpu.VMEM((n_epochs, LANES), jnp.float32),
        ],
        compiler_params=pltpu.CompilerParams(vmem_limit_bytes=40 * 1024 * 1024),
        name="terms",
    )(pairs_t, data, pairs_t, slots)
    parts = [
        part_k if k == 0 else lax.ppermute(part_k, "pair", [(i, (i + k) % n_pair) for i in range(n_pair)])
        for k, part_k in enumerate(parts)
    ]
    return pl.pallas_call(
        place_kernel,
        out_shape=(
            jax.ShapeDtypeStruct((n_epochs // n_pair, tiles_dev, 2, LANES), jnp.float32),
            jax.ShapeDtypeStruct((n_pairs // 2, tiles_dev, LANES), jnp.float32),
        ),
        in_specs=[vector] * n_pair,
        out_specs=(vector, vector),
        compiler_params=pltpu.CompilerParams(vmem_limit_bytes=8 * 1024 * 1024),
        name="place",
    )(*parts)


def solution(mesh):
    placed = (P("tile", None, None, None), P(), P(), P())
    return jax.shard_map(
        local,
        mesh=mesh,
        in_specs=placed,
        out_specs=(P("pair", "tile", None, None), P("pair", "tile", None)),
        check_vma=False,
    )
```

```python
import functools

import jax
import jax.numpy as jnp
from jax import lax
from jax.experimental import pallas as pl
from jax.experimental.pallas import tpu as pltpu
from jax.sharding import PartitionSpec as P

EPS = 1e-06
LOOK_PIXELS = 64
LANES = 128
BATCH = 8


def split_dot(ones, x):
    high = x.astype(jnp.bfloat16)
    rest = x - high.astype(jnp.float32)
    middle = rest.astype(jnp.bfloat16)
    low = (rest - middle.astype(jnp.float32)).astype(jnp.bfloat16)
    width = x.shape[1]
    out = jnp.dot(ones, jnp.concatenate([high, middle, low], axis=1), preferred_element_type=jnp.float32)
    return out[:, :width] + out[:, width : 2 * width] + out[:, 2 * width :]


def dot_split(x, ones):
    high = x.astype(jnp.bfloat16)
    rest = x - high.astype(jnp.float32)
    middle = rest.astype(jnp.bfloat16)
    low = (rest - middle.astype(jnp.float32)).astype(jnp.bfloat16)
    rows = x.shape[0]
    out = jnp.dot(jnp.concatenate([high, middle, low], axis=0), ones, preferred_element_type=jnp.float32)
    return out[:rows] + out[rows : 2 * rows] + out[2 * rows :]


def order_kernel(source_ref, slc_ref, held, in_sem):
    n_dev, _, tiles_dev, _, part = held.shape
    n_chunks = in_sem.shape[0]
    chunk = n_dev // n_chunks
    start = pl.multiple_of(lax.axis_index("pair") * part, part)

    for c in range(n_chunks):

        @pl.loop(c * chunk, (c + 1) * chunk, unroll=4)
        def _(d):
            for k in range(tiles_dev):
                src = source_ref[d * tiles_dev + k]
                pltpu.make_async_copy(
                    slc_ref.at[:, src, :, pl.ds(start, part)], held.at[d, :, k], in_sem.at[c]
                ).start()

    for c in range(n_chunks):
        at = pl.ds(c * chunk, chunk)
        pltpu.make_async_copy(held.at[at], held.at[at], in_sem.at[c]).wait()


def terms_kernel(pairs_sm, data_ref, pairs_ref, groups_ref, *refs):
    out_refs, (wide, norm, gamma, chosen_ref, rhs_ref) = refs[:-5], refs[-5:]
    n_epochs = data_ref.shape[0]
    n_pairs = pairs_ref.shape[1]
    step = wide.shape[0]
    sub = lax.broadcasted_iota(jnp.int32, (8, LANES), 0)
    lane = lax.broadcasted_iota(jnp.int32, (8, LANES), 1)
    first = sub < 4
    rows_i = lax.broadcasted_iota(jnp.int32, (LANES, LANES), 0)
    cols_i = lax.broadcasted_iota(jnp.int32, (LANES, LANES), 1)
    same_look = (rows_i // 16 == cols_i // 16).astype(jnp.bfloat16)

    @pl.loop(0, n_epochs // step, unroll=4)
    def _(block):
        at = pl.ds(block * step, step)
        wide[...] = data_ref[at].astype(jnp.float32)
        re = wide[:, :, pl.ds(0, 16, stride=2), :]
        im = wide[:, :, pl.ds(1, 16, stride=2), :]
        power = re * re + im * im
        lines = power[:, :, 0:8] + power[:, :, 8:16]
        lines = lines + pltpu.roll(lines, 4, 2)
        level = dot_split(lines.reshape(step * 2 * 8, LANES), same_look).reshape(step, 2, 8, LANES)
        inv = lax.rsqrt(level * (1.0 / LOOK_PIXELS) + EPS) * 0.125
        inv = jnp.concatenate([inv, inv], axis=2)
        norm[at, 0] = re * inv
        norm[at, 1] = im * inv

    @pl.loop(0, n_pairs // BATCH, unroll=8)
    def _(batch):
        def one(j):
            q = batch * BATCH + j
            r = pairs_sm[0, q]
            t = pairs_sm[1, q]
            a_re, a_im = norm[r, 0], norm[r, 1]
            b_re, b_im = norm[t, 0], norm[t, 1]
            parts = []
            for cross in (a_re * b_re + a_im * b_im, a_im * b_re - a_re * b_im):
                s0 = cross[0, 0:8] + cross[0, 8:16]
                s1 = cross[1, 0:8] + cross[1, 8:16]
                parts.append(jnp.where(first, s0, s1) + pltpu.roll(jnp.where(first, s1, s0), 4, 0))
            return merge(parts[0], parts[1], 8)

        def merge(a, b, k):
            return jnp.where(
                (lane & k) == 0, a + pltpu.roll(a, LANES - k, 1), b + pltpu.roll(b, k, 1)
            )

        def tree(js, k):
            if len(js) == 1:
                return one(js[0])
            return merge(tree([j for j in js if not j & k], k // 2), tree([j for j in js if j & k], k // 2), k)

        z = tree(list(range(BATCH)), 4)
        gamma[batch] = z

    z = gamma[...]
    sub = lax.broadcasted_iota(jnp.int32, z.shape, 1)
    lane = lax.broadcasted_iota(jnp.int32, z.shape, 2)
    for k in (4, 2, 1):
        up = pltpu.roll(pltpu.roll(z, k, 2), 8 - k, 1)
        down = pltpu.roll(pltpu.roll(z, LANES - k, 2), k, 1)
        low_row, low_lane = (sub & k) == 0, (lane & k) == 0
        z = jnp.where(low_row == low_lane, z, jnp.where(low_row, up, down))
    z = z.reshape(n_pairs, LANES)
    comp0 = (lax.broadcasted_iota(jnp.int32, z.shape, 1) & 8) == 0
    square = z * z
    weight = square + jnp.where(comp0, pltpu.roll(square, LANES - 8, 1), pltpu.roll(square, 8, 1))
    refs, secs = pairs_ref[0:1, :], pairs_ref[1:2, :]
    epochs = lax.broadcasted_iota(jnp.int32, (n_epochs, n_pairs), 0)
    incidence = (epochs == secs).astype(jnp.float32) - (epochs == refs).astype(jnp.float32)
    rhs_ref[...] = split_dot(incidence.astype(jnp.bfloat16), weight * z)
    groups = groups_ref[0:1, :]
    mine = (lax.broadcasted_iota(jnp.int32, (8, n_pairs), 0) == groups).astype(jnp.float32)
    before = (
        lax.broadcasted_iota(jnp.int32, (n_pairs, n_pairs), 0)
        < lax.broadcasted_iota(jnp.int32, (n_pairs, n_pairs), 1)
    )
    ranks = jnp.dot(
        mine.astype(jnp.bfloat16), before.astype(jnp.bfloat16), preferred_element_type=jnp.float32
    )
    rank = jnp.sum(mine * ranks, axis=0, keepdims=True).astype(jnp.int32)
    half = n_pairs // 4
    slot = jnp.where(rank < half, groups * half + rank, n_pairs + groups * half + rank - half)
    hit = (lax.broadcasted_iota(jnp.int32, (2 * n_pairs, n_pairs), 0) == slot).astype(jnp.bfloat16)
    chosen = split_dot(hit, weight)
    chosen_ref[...] = jnp.where(comp0, chosen[:n_pairs], chosen[n_pairs:])
    n_members = len(out_refs)
    half, e_out = n_pairs // n_members, n_epochs // n_members
    me = lax.axis_index("pair")
    for k, out_ref in enumerate(out_refs):
        to = lax.rem(me + k, n_members)
        out_ref[0:half, :] = chosen_ref[pl.ds(pl.multiple_of(to * half, half), half), :]
        out_ref[half : half + e_out, :] = rhs_ref[pl.ds(pl.multiple_of(to * e_out, e_out), e_out), :]


def place_kernel(*refs):
    part_refs, (rhs_ref, coherence_ref) = refs[:-2], refs[-2:]
    n_members = len(part_refs)
    rows = part_refs[0].shape[0]
    half = coherence_ref.shape[0] // 2
    width = LANES // n_members
    me = lax.axis_index("pair")
    i = lax.broadcasted_iota(jnp.int32, (LANES, LANES), 0)
    j = lax.broadcasted_iota(jnp.int32, (LANES, LANES), 1)
    ones = (j == (i % 16) * 8 + i // 16).astype(jnp.bfloat16)
    parts = dot_split(jnp.concatenate([r[...] for r in part_refs], axis=0), ones)
    owner = lax.broadcasted_iota(jnp.int32, (rows, LANES), 1) // width
    total = [None] * 4
    for k in range(n_members):
        member = lax.rem(me + n_members - k, n_members)
        own = owner == member
        base = pltpu.roll(parts[k * rows : (k + 1) * rows], member * width, 1)
        for g in range(4):
            piece = base if g == 0 else pltpu.roll(base, LANES - g * width, 1)
            total[g] = piece if k == 0 else jnp.where(own, piece, total[g])
    for comp in range(2):
        for slot in range(2):
            coherence_ref[pl.ds(comp * half, half), slot, :] = total[comp * 2 + slot][:half]
            rhs_ref[:, slot, comp, :] = total[comp * 2 + slot][half:]


def local(slc, pairs, groups, tile_source):
    n_tile, n_pair = lax.axis_size("tile"), lax.axis_size("pair")
    e_dev, n_tiles, _, pixels = slc.shape
    tiles_dev = n_tiles // n_tile
    part = pixels // n_pair
    n_pairs = pairs.shape[0]
    n_epochs = e_dev * n_tile
    in_hbm = pl.BlockSpec(memory_space=pltpu.HBM)
    scalars = pl.BlockSpec(memory_space=pltpu.SMEM)
    vector = pl.BlockSpec(memory_space=pltpu.VMEM)
    pairs_t, groups_t = pairs.T, groups.reshape(1, n_pairs)
    out_shape = (n_tile, e_dev, tiles_dev, 2, part)
    chunks = 4
    ordered = pl.pallas_call(
        order_kernel,
        out_shape=jax.ShapeDtypeStruct(out_shape, slc.dtype),
        in_specs=[scalars, in_hbm],
        out_specs=vector,
        scratch_shapes=[
            pltpu.SemaphoreType.DMA((chunks,)),
        ],
        compiler_params=pltpu.CompilerParams(vmem_limit_bytes=48 * 1024 * 1024),
        name="order",
    )(tile_source, slc)
    data = lax.all_to_all(ordered, "tile", split_axis=0, concat_axis=0, tiled=True)
    data = data.reshape(n_epochs, tiles_dev, 2, part // LANES, LANES)
    data = jnp.swapaxes(data, 2, 3).reshape(n_epochs, tiles_dev, 2 * part // LANES, LANES)
    rows = n_pairs // 4 + n_epochs // n_pair
    parts = pl.pallas_call(
        terms_kernel,
        out_shape=[jax.ShapeDtypeStruct((rows, LANES), jnp.float32)] * n_pair,
        in_specs=[scalars, vector, vector, vector],
        out_specs=[vector] * n_pair,
        scratch_shapes=[
            pltpu.VMEM((8, tiles_dev, 32, LANES), jnp.float32),
            pltpu.VMEM((n_epochs, 2, tiles_dev, 16, LANES), jnp.float32),
            pltpu.VMEM((n_pairs // BATCH, BATCH, LANES), jnp.float32),
            pltpu.VMEM((n_pairs, LANES), jnp.float32),
            pltpu.VMEM((n_epochs, LANES), jnp.float32),
        ],
        compiler_params=pltpu.CompilerParams(vmem_limit_bytes=40 * 1024 * 1024),
        name="terms",
    )(pairs_t, data, pairs_t, groups_t)
    parts = [
        part_k if k == 0 else lax.ppermute(part_k, "pair", [(i, (i + k) % n_pair) for i in range(n_pair)])
        for k, part_k in enumerate(parts)
    ]
    return pl.pallas_call(
        place_kernel,
        out_shape=(
            jax.ShapeDtypeStruct((n_epochs // n_pair, tiles_dev, 2, LANES), jnp.float32),
            jax.ShapeDtypeStruct((n_pairs // 2, tiles_dev, LANES), jnp.float32),
        ),
        in_specs=[vector] * n_pair,
        out_specs=(vector, vector),
        compiler_params=pltpu.CompilerParams(vmem_limit_bytes=8 * 1024 * 1024),
        name="place",
    )(*parts)


def solution(mesh):
    placed = (P("tile", None, None, None), P(), P(), P())
    return jax.shard_map(
        local,
        mesh=mesh,
        in_specs=placed,
        out_specs=(P("pair", "tile", None, None), P("pair", "tile", None)),
        check_vma=False,
    )
```

```python
import functools

import jax
import jax.numpy as jnp
from jax import lax
from jax.experimental import pallas as pl
from jax.experimental.pallas import tpu as pltpu
from jax.sharding import PartitionSpec as P

EPS = 1e-06
LOOK_PIXELS = 64
LANES = 128
BATCH = 8


def split_dot(ones, x):
    high = x.astype(jnp.bfloat16)
    rest = x - high.astype(jnp.float32)
    middle = rest.astype(jnp.bfloat16)
    low = (rest - middle.astype(jnp.float32)).astype(jnp.bfloat16)
    width = x.shape[1]
    out = jnp.dot(ones, jnp.concatenate([high, middle, low], axis=1), preferred_element_type=jnp.float32)
    return out[:, :width] + out[:, width : 2 * width] + out[:, 2 * width :]


def dot_split(x, ones):
    high = x.astype(jnp.bfloat16)
    rest = x - high.astype(jnp.float32)
    middle = rest.astype(jnp.bfloat16)
    low = (rest - middle.astype(jnp.float32)).astype(jnp.bfloat16)
    rows = x.shape[0]
    out = jnp.dot(jnp.concatenate([high, middle, low], axis=0), ones, preferred_element_type=jnp.float32)
    return out[:rows] + out[rows : 2 * rows] + out[2 * rows :]


def order_kernel(source_ref, slc_ref, held, in_sem):
    n_dev, _, tiles_dev, _, part = held.shape
    n_chunks = in_sem.shape[0]
    chunk = n_dev // n_chunks
    start = pl.multiple_of(lax.axis_index("pair") * part, part)

    for c in range(n_chunks):

        @pl.loop(c * chunk, (c + 1) * chunk, unroll=4)
        def _(d):
            for k in range(tiles_dev):
                src = source_ref[d * tiles_dev + k]
                pltpu.make_async_copy(
                    slc_ref.at[:, src, :, pl.ds(start, part)], held.at[d, :, k], in_sem.at[c]
                ).start()

    for c in range(n_chunks):
        at = pl.ds(c * chunk, chunk)
        pltpu.make_async_copy(held.at[at], held.at[at], in_sem.at[c]).wait()


def terms_kernel(data_ref, pairs_ref, groups_ref, *refs):
    out_refs, (wide, norm, gamma, chosen_ref, rhs_ref, pairs_sm, sem) = refs[:-7], refs[-7:]
    pairs_copy = pltpu.make_async_copy(pairs_ref, pairs_sm, sem)
    pairs_copy.start()
    n_epochs = data_ref.shape[0]
    n_pairs = pairs_ref.shape[1]
    step = wide.shape[0]
    sub = lax.broadcasted_iota(jnp.int32, (8, LANES), 0)
    lane = lax.broadcasted_iota(jnp.int32, (8, LANES), 1)
    first = sub < 4
    rows_i = lax.broadcasted_iota(jnp.int32, (2 * LANES, LANES), 0)
    cols_i = lax.broadcasted_iota(jnp.int32, (2 * LANES, LANES), 1)
    same_look = ((rows_i % LANES) // 16 == cols_i // 16).astype(jnp.bfloat16)

    @pl.loop(0, n_epochs // step, unroll=4)
    def _(block):
        at = pl.ds(block * step, step)
        wide[...] = data_ref[at].astype(jnp.float32)
        re = wide[:, :, pl.ds(0, 16, stride=2), :]
        im = wide[:, :, pl.ds(1, 16, stride=2), :]
        power = re * re + im * im
        lines = power[:, :, 0:8] + power[:, :, 8:16]
        lines = jnp.where(first, lines[:, 0], lines[:, 1]) + pltpu.roll(
            jnp.where(first, lines[:, 1], lines[:, 0]), 4, 1
        )
        lines = lines.reshape(step * 8, LANES)
        high = lines.astype(jnp.bfloat16)
        low = (lines - high.astype(jnp.float32)).astype(jnp.bfloat16)
        level = jnp.dot(
            jnp.concatenate([high, low], axis=1), same_look, preferred_element_type=jnp.float32
        ).reshape(step, 8, LANES)
        inv = lax.rsqrt(level * (1.0 / LOOK_PIXELS) + EPS) * 0.125
        swapped = pltpu.roll(inv, 4, 1)
        for k, inv_k in enumerate((jnp.where(first, inv, swapped), jnp.where(first, swapped, inv))):
            inv_k = jnp.concatenate([inv_k, inv_k], axis=1)
            norm[at, 0, k] = re[:, k] * inv_k
            norm[at, 1, k] = im[:, k] * inv_k

    pairs_copy.wait()

    @pl.loop(0, n_pairs // BATCH, unroll=8)
    def _(batch):
        def one(j):
            q = batch * BATCH + j
            r = pairs_sm[0, q]
            t = pairs_sm[1, q]
            a_re, a_im = norm[r, 0], norm[r, 1]
            b_re, b_im = norm[t, 0], norm[t, 1]
            parts = []
            for cross in (a_re * b_re + a_im * b_im, a_im * b_re - a_re * b_im):
                s0 = cross[0, 0:8] + cross[0, 8:16]
                s1 = cross[1, 0:8] + cross[1, 8:16]
                parts.append(jnp.where(first, s0, s1) + pltpu.roll(jnp.where(first, s1, s0), 4, 0))
            return merge(parts[0], parts[1], 8)

        def merge(a, b, k):
            return jnp.where(
                (lane & k) == 0, a + pltpu.roll(a, LANES - k, 1), b + pltpu.roll(b, k, 1)
            )

        def tree(js, k):
            if len(js) == 1:
                return one(js[0])
            return merge(tree([j for j in js if not j & k], k // 2), tree([j for j in js if j & k], k // 2), k)

        z = tree(list(range(BATCH)), 4)
        gamma[batch] = z

    z = gamma[...]
    sub = lax.broadcasted_iota(jnp.int32, z.shape, 1)
    lane = lax.broadcasted_iota(jnp.int32, z.shape, 2)
    for k in (4, 2, 1):
        up = pltpu.roll(pltpu.roll(z, k, 2), 8 - k, 1)
        down = pltpu.roll(pltpu.roll(z, LANES - k, 2), k, 1)
        low_row, low_lane = (sub & k) == 0, (lane & k) == 0
        z = jnp.where(low_row == low_lane, z, jnp.where(low_row, up, down))
    z = z.reshape(n_pairs, LANES)
    comp0 = (lax.broadcasted_iota(jnp.int32, z.shape, 1) & 8) == 0
    square = z * z
    weight = square + jnp.where(comp0, pltpu.roll(square, LANES - 8, 1), pltpu.roll(square, 8, 1))
    refs, secs = pairs_ref[0:1, :], pairs_ref[1:2, :]
    epochs = lax.broadcasted_iota(jnp.int32, (n_epochs, n_pairs), 0)
    incidence = (epochs == secs).astype(jnp.float32) - (epochs == refs).astype(jnp.float32)
    rhs_ref[...] = split_dot(incidence.astype(jnp.bfloat16), weight * z)
    groups = groups_ref[0:1, :]
    mine = (lax.broadcasted_iota(jnp.int32, (8, n_pairs), 0) == groups).astype(jnp.float32)
    before = (
        lax.broadcasted_iota(jnp.int32, (n_pairs, n_pairs), 0)
        < lax.broadcasted_iota(jnp.int32, (n_pairs, n_pairs), 1)
    )
    ranks = jnp.dot(
        mine.astype(jnp.bfloat16), before.astype(jnp.bfloat16), preferred_element_type=jnp.float32
    )
    rank = jnp.sum(mine * ranks, axis=0, keepdims=True).astype(jnp.int32)
    half = n_pairs // 4
    slot = jnp.where(rank < half, groups * half + rank, n_pairs + groups * half + rank - half)
    hit = (lax.broadcasted_iota(jnp.int32, (2 * n_pairs, n_pairs), 0) == slot).astype(jnp.bfloat16)
    high = weight.astype(jnp.bfloat16).astype(jnp.float32)
    middle = (weight - high).astype(jnp.bfloat16).astype(jnp.float32)
    three = jnp.concatenate([jnp.where(comp0, high, middle), (weight - high) - middle], axis=1)
    chosen = jnp.dot(hit, three.astype(jnp.bfloat16), preferred_element_type=jnp.float32)
    first_half = chosen[:n_pairs, :LANES] + pltpu.roll(chosen[:n_pairs, :LANES], LANES - 8, 1)
    last_half = chosen[n_pairs:, :LANES] + pltpu.roll(chosen[n_pairs:, :LANES], 8, 1)
    chosen_ref[...] = jnp.where(
        comp0, first_half + chosen[:n_pairs, LANES:], last_half + chosen[n_pairs:, LANES:]
    )
    n_members = len(out_refs)
    half, e_out = n_pairs // n_members, n_epochs // n_members
    me = lax.axis_index("pair")
    for k, out_ref in enumerate(out_refs):
        to = lax.rem(me + k, n_members)
        out_ref[0:half, :] = chosen_ref[pl.ds(pl.multiple_of(to * half, half), half), :]
        out_ref[half : half + e_out, :] = rhs_ref[pl.ds(pl.multiple_of(to * e_out, e_out), e_out), :]


def place_kernel(*refs):
    part_refs, (rhs_ref, coherence_ref) = refs[:-2], refs[-2:]
    n_members = len(part_refs)
    rows = part_refs[0].shape[0]
    half = coherence_ref.shape[0] // 2
    width = LANES // n_members
    me = lax.axis_index("pair")
    i = lax.broadcasted_iota(jnp.int32, (LANES, LANES), 0)
    j = lax.broadcasted_iota(jnp.int32, (LANES, LANES), 1)
    ones = (j == (i % 16) * 8 + i // 16).astype(jnp.bfloat16)
    parts = dot_split(jnp.concatenate([r[...] for r in part_refs], axis=0), ones)
    owner = lax.broadcasted_iota(jnp.int32, (rows, LANES), 1) // width
    total = [None] * 4
    for k in range(n_members):
        member = lax.rem(me + n_members - k, n_members)
        own = owner == member
        base = pltpu.roll(parts[k * rows : (k + 1) * rows], member * width, 1)
        for g in range(4):
            piece = base if g == 0 else pltpu.roll(base, LANES - g * width, 1)
            total[g] = piece if k == 0 else jnp.where(own, piece, total[g])
    for comp in range(2):
        for slot in range(2):
            coherence_ref[pl.ds(comp * half, half), slot, :] = total[comp * 2 + slot][:half]
            rhs_ref[:, slot, comp, :] = total[comp * 2 + slot][half:]


def local(slc, pairs, groups, tile_source):
    n_tile, n_pair = lax.axis_size("tile"), lax.axis_size("pair")
    e_dev, n_tiles, _, pixels = slc.shape
    tiles_dev = n_tiles // n_tile
    part = pixels // n_pair
    n_pairs = pairs.shape[0]
    n_epochs = e_dev * n_tile
    in_hbm = pl.BlockSpec(memory_space=pltpu.HBM)
    scalars = pl.BlockSpec(memory_space=pltpu.SMEM)
    vector = pl.BlockSpec(memory_space=pltpu.VMEM)
    pairs_t, groups_t = pairs.T, groups.reshape(1, n_pairs)
    out_shape = (n_tile, e_dev, tiles_dev, 2, part)
    chunks = 4
    ordered = pl.pallas_call(
        order_kernel,
        out_shape=jax.ShapeDtypeStruct(out_shape, slc.dtype),
        in_specs=[scalars, in_hbm],
        out_specs=vector,
        scratch_shapes=[
            pltpu.SemaphoreType.DMA((chunks,)),
        ],
        compiler_params=pltpu.CompilerParams(vmem_limit_bytes=48 * 1024 * 1024),
        name="order",
    )(tile_source, slc)
    data = lax.all_to_all(ordered, "tile", split_axis=0, concat_axis=0, tiled=True)
    data = data.reshape(n_epochs, tiles_dev, 2, part // LANES, LANES)
    data = jnp.swapaxes(data, 2, 3).reshape(n_epochs, tiles_dev, 2 * part // LANES, LANES)
    rows = n_pairs // 4 + n_epochs // n_pair
    parts = list(pl.pallas_call(
        terms_kernel,
        out_shape=[jax.ShapeDtypeStruct((rows, LANES), jnp.float32)] * n_pair,
        in_specs=[vector, vector, vector],
        out_specs=[vector] * n_pair,
        scratch_shapes=[
            pltpu.VMEM((8, tiles_dev, 32, LANES), jnp.float32),
            pltpu.VMEM((n_epochs, 2, tiles_dev, 16, LANES), jnp.float32),
            pltpu.VMEM((n_pairs // BATCH, BATCH, LANES), jnp.float32),
            pltpu.VMEM((n_pairs, LANES), jnp.float32),
            pltpu.VMEM((n_epochs, LANES), jnp.float32),
            pltpu.SMEM(pairs_t.shape, jnp.int32),
            pltpu.SemaphoreType.DMA,
        ],
        compiler_params=pltpu.CompilerParams(vmem_limit_bytes=40 * 1024 * 1024),
        name="terms",
    )(data, pairs_t, groups_t))
    ring = range(n_pair)
    for k in sorted(ring, key=lambda k: -min(k, n_pair - k)):
        if k:
            parts[k] = lax.ppermute(parts[k], "pair", [(i, (i + k) % n_pair) for i in ring])
    return pl.pallas_call(
        place_kernel,
        out_shape=(
            jax.ShapeDtypeStruct((n_epochs // n_pair, tiles_dev, 2, LANES), jnp.float32),
            jax.ShapeDtypeStruct((n_pairs // 2, tiles_dev, LANES), jnp.float32),
        ),
        in_specs=[vector] * n_pair,
        out_specs=(vector, vector),
        compiler_params=pltpu.CompilerParams(vmem_limit_bytes=8 * 1024 * 1024),
        name="place",
    )(*parts)


def solution(mesh):
    placed = (P("tile", None, None, None), P(), P(), P())
    return jax.shard_map(
        local,
        mesh=mesh,
        in_specs=placed,
        out_specs=(P("pair", "tile", None, None), P("pair", "tile", None)),
        check_vma=False,
    )
```

```python
import functools

import jax
import jax.numpy as jnp
from jax import lax
from jax.experimental import pallas as pl
from jax.experimental.pallas import tpu as pltpu
from jax.sharding import PartitionSpec as P

EPS = 1e-06
LOOK_PIXELS = 64
LANES = 128
BATCH = 8


def split_dot(ones, x):
    high = x.astype(jnp.bfloat16)
    rest = x - high.astype(jnp.float32)
    middle = rest.astype(jnp.bfloat16)
    low = (rest - middle.astype(jnp.float32)).astype(jnp.bfloat16)
    width = x.shape[1]
    out = jnp.dot(ones, jnp.concatenate([high, middle, low], axis=1), preferred_element_type=jnp.float32)
    return out[:, :width] + out[:, width : 2 * width] + out[:, 2 * width :]


def across(x, lanes):
    return jnp.take_along_axis(x, lanes, axis=x.ndim - 1, mode="promise_in_bounds")


def order_kernel(source_ref, slc_ref, held, in_sem):
    n_dev, _, tiles_dev, _, part = held.shape
    n_chunks = in_sem.shape[0]
    chunk = n_dev // n_chunks
    start = pl.multiple_of(lax.axis_index("pair") * part, part)

    for c in range(n_chunks):

        @pl.loop(c * chunk, (c + 1) * chunk, unroll=4)
        def _(d):
            for k in range(tiles_dev):
                src = source_ref[d * tiles_dev + k]
                pltpu.make_async_copy(
                    slc_ref.at[:, src, :, pl.ds(start, part)], held.at[d, :, k], in_sem.at[c]
                ).start()

    for c in range(n_chunks):
        at = pl.ds(c * chunk, chunk)
        pltpu.make_async_copy(held.at[at], held.at[at], in_sem.at[c]).wait()


def terms_kernel(data_ref, pairs_ref, groups_ref, *refs):
    out_refs, (wide, norm, gamma, chosen_ref, rhs_ref, pairs_sm, sem) = refs[:-7], refs[-7:]
    pairs_copy = pltpu.make_async_copy(pairs_ref, pairs_sm, sem)
    pairs_copy.start()
    n_epochs = data_ref.shape[0]
    n_pairs = pairs_ref.shape[1]
    step = wide.shape[0]
    sub = lax.broadcasted_iota(jnp.int32, (8, LANES), 0)
    lane = lax.broadcasted_iota(jnp.int32, (8, LANES), 1)
    first = sub < 4
    rows_i = lax.broadcasted_iota(jnp.int32, (2 * LANES, LANES), 0)
    cols_i = lax.broadcasted_iota(jnp.int32, (2 * LANES, LANES), 1)
    same_look = ((rows_i % LANES) // 16 == cols_i // 16).astype(jnp.bfloat16)

    @pl.loop(0, n_epochs // step, unroll=8)
    def _(block):
        at = pl.ds(block * step, step)
        wide[...] = data_ref[at].astype(jnp.float32)
        re = wide[:, :, pl.ds(0, 16, stride=2), :]
        im = wide[:, :, pl.ds(1, 16, stride=2), :]
        power = re * re + im * im
        lines = power[:, :, 0:8] + power[:, :, 8:16]
        lines = jnp.where(first, lines[:, 0], lines[:, 1]) + pltpu.roll(
            jnp.where(first, lines[:, 1], lines[:, 0]), 4, 1
        )
        lines = lines.reshape(step * 8, LANES)
        high = lines.astype(jnp.bfloat16)
        low = (lines - high.astype(jnp.float32)).astype(jnp.bfloat16)
        level = jnp.dot(
            jnp.concatenate([high, low], axis=1), same_look, preferred_element_type=jnp.float32
        ).reshape(step, 8, LANES)
        inv = lax.rsqrt(level * (1.0 / LOOK_PIXELS) + EPS) * 0.125
        swapped = pltpu.roll(inv, 4, 1)
        for k, inv_k in enumerate((jnp.where(first, inv, swapped), jnp.where(first, swapped, inv))):
            inv_k = jnp.concatenate([inv_k, inv_k], axis=1)
            norm[at, 0, k] = re[:, k] * inv_k
            norm[at, 1, k] = im[:, k] * inv_k

    pairs_copy.wait()

    @pl.loop(0, n_pairs // BATCH, unroll=8)
    def _(batch):
        def one(j):
            q = batch * BATCH + j
            r = pairs_sm[0, q]
            t = pairs_sm[1, q]
            a_re, a_im = norm[r, 0], norm[r, 1]
            b_re, b_im = norm[t, 0], norm[t, 1]
            parts = []
            for cross in (a_re * b_re + a_im * b_im, a_im * b_re - a_re * b_im):
                s0 = cross[0, 0:8] + cross[0, 8:16]
                s1 = cross[1, 0:8] + cross[1, 8:16]
                parts.append(jnp.where(first, s0, s1) + pltpu.roll(jnp.where(first, s1, s0), 4, 0))
            return merge(parts[0], parts[1], 8)

        def merge(a, b, k):
            own = (lane & k) == 0
            return jnp.where(own, a, b) + across(jnp.where(own, b, a), lane ^ k)

        def tree(js, k):
            if len(js) == 1:
                return one(js[0])
            return merge(tree([j for j in js if not j & k], k // 2), tree([j for j in js if j & k], k // 2), k)

        z = tree(list(range(BATCH)), 4)
        gamma[batch] = z

    z = gamma[...]
    sub = lax.broadcasted_iota(jnp.int32, z.shape, 1)
    lane = lax.broadcasted_iota(jnp.int32, z.shape, 2)
    for k in (4, 2, 1):
        low_row = (sub & k) == 0
        moved = across(z.reshape(n_pairs, LANES), (lane ^ k).reshape(n_pairs, LANES)).reshape(z.shape)
        up, down = pltpu.roll(moved, 8 - k, 1), pltpu.roll(moved, k, 1)
        z = jnp.where(low_row == ((lane & k) == 0), z, jnp.where(low_row, up, down))
    z = z.reshape(n_pairs, LANES)
    comp0 = (lax.broadcasted_iota(jnp.int32, z.shape, 1) & 8) == 0
    square = z * z
    weight = square + jnp.where(comp0, pltpu.roll(square, LANES - 8, 1), pltpu.roll(square, 8, 1))
    refs, secs = pairs_ref[0:1, :], pairs_ref[1:2, :]
    epochs = lax.broadcasted_iota(jnp.int32, (n_epochs, n_pairs), 0)
    incidence = (epochs == secs).astype(jnp.float32) - (epochs == refs).astype(jnp.float32)
    rhs_ref[...] = split_dot(incidence.astype(jnp.bfloat16), weight * z)
    groups = groups_ref[0:1, :]
    mine = (lax.broadcasted_iota(jnp.int32, (8, n_pairs), 0) == groups).astype(jnp.float32)
    before = (
        lax.broadcasted_iota(jnp.int32, (n_pairs, n_pairs), 0)
        < lax.broadcasted_iota(jnp.int32, (n_pairs, n_pairs), 1)
    )
    ranks = jnp.dot(
        mine.astype(jnp.bfloat16), before.astype(jnp.bfloat16), preferred_element_type=jnp.float32
    )
    rank = jnp.sum(mine * ranks, axis=0, keepdims=True).astype(jnp.int32)
    half = n_pairs // 4
    slot = jnp.where(rank < half, groups * half + rank, n_pairs + groups * half + rank - half)
    hit = (lax.broadcasted_iota(jnp.int32, (2 * n_pairs, n_pairs), 0) == slot).astype(jnp.bfloat16)
    high = weight.astype(jnp.bfloat16).astype(jnp.float32)
    middle = (weight - high).astype(jnp.bfloat16).astype(jnp.float32)
    three = jnp.concatenate([jnp.where(comp0, high, middle), (weight - high) - middle], axis=1)
    chosen = jnp.dot(hit, three.astype(jnp.bfloat16), preferred_element_type=jnp.float32)
    first_half = chosen[:n_pairs, :LANES] + pltpu.roll(chosen[:n_pairs, :LANES], LANES - 8, 1)
    last_half = chosen[n_pairs:, :LANES] + pltpu.roll(chosen[n_pairs:, :LANES], 8, 1)
    chosen_ref[...] = jnp.where(
        comp0, first_half + chosen[:n_pairs, LANES:], last_half + chosen[n_pairs:, LANES:]
    )
    n_members = len(out_refs)
    half, e_out = n_pairs // n_members, n_epochs // n_members
    me = lax.axis_index("pair")
    for k, out_ref in enumerate(out_refs):
        to = lax.rem(me + k, n_members)
        out_ref[0:half, :] = chosen_ref[pl.ds(pl.multiple_of(to * half, half), half), :]
        out_ref[half : half + e_out, :] = rhs_ref[pl.ds(pl.multiple_of(to * e_out, e_out), e_out), :]


def place_kernel(*refs):
    part_refs, (rhs_ref, coherence_ref) = refs[:-2], refs[-2:]
    n_members = len(part_refs)
    rows = part_refs[0].shape[0]
    half = coherence_ref.shape[0] // 2
    width = LANES // n_members
    me = lax.axis_index("pair")
    lane = lax.broadcasted_iota(jnp.int32, (rows, LANES), 1)
    look = lane % width
    source = (look % 8) * 16 + look // 8
    owner = lane // width
    total = [None] * 4
    for k, part_ref in enumerate(part_refs):
        own = owner == lax.rem(me + n_members - k, n_members)
        part = part_ref[...]
        for g in range(4):
            piece = across(part, source + 4 * g)
            total[g] = piece if k == 0 else jnp.where(own, piece, total[g])
    for comp in range(2):
        for slot in range(2):
            coherence_ref[pl.ds(comp * half, half), slot, :] = total[comp * 2 + slot][:half]
            rhs_ref[:, slot, comp, :] = total[comp * 2 + slot][half:]


def local(slc, pairs, groups, tile_source):
    n_tile, n_pair = lax.axis_size("tile"), lax.axis_size("pair")
    e_dev, n_tiles, _, pixels = slc.shape
    tiles_dev = n_tiles // n_tile
    part = pixels // n_pair
    n_pairs = pairs.shape[0]
    n_epochs = e_dev * n_tile
    in_hbm = pl.BlockSpec(memory_space=pltpu.HBM)
    scalars = pl.BlockSpec(memory_space=pltpu.SMEM)
    vector = pl.BlockSpec(memory_space=pltpu.VMEM)
    pairs_t, groups_t = pairs.T, groups.reshape(1, n_pairs)
    out_shape = (n_tile, e_dev, tiles_dev, 2, part)
    chunks = 4
    ordered = pl.pallas_call(
        order_kernel,
        out_shape=jax.ShapeDtypeStruct(out_shape, slc.dtype),
        in_specs=[scalars, in_hbm],
        out_specs=vector,
        scratch_shapes=[
            pltpu.SemaphoreType.DMA((chunks,)),
        ],
        compiler_params=pltpu.CompilerParams(vmem_limit_bytes=48 * 1024 * 1024),
        name="order",
    )(tile_source, slc)
    data = lax.all_to_all(ordered, "tile", split_axis=0, concat_axis=0, tiled=True)
    data = data.reshape(n_epochs, tiles_dev, 2, part // LANES, LANES)
    data = jnp.swapaxes(data, 2, 3).reshape(n_epochs, tiles_dev, 2 * part // LANES, LANES)
    rows = n_pairs // 4 + n_epochs // n_pair
    parts = list(pl.pallas_call(
        terms_kernel,
        out_shape=[jax.ShapeDtypeStruct((rows, LANES), jnp.float32)] * n_pair,
        in_specs=[vector, vector, vector],
        out_specs=[vector] * n_pair,
        scratch_shapes=[
            pltpu.VMEM((8, tiles_dev, 32, LANES), jnp.float32),
            pltpu.VMEM((n_epochs, 2, tiles_dev, 16, LANES), jnp.float32),
            pltpu.VMEM((n_pairs // BATCH, BATCH, LANES), jnp.float32),
            pltpu.VMEM((n_pairs, LANES), jnp.float32),
            pltpu.VMEM((n_epochs, LANES), jnp.float32),
            pltpu.SMEM(pairs_t.shape, jnp.int32),
            pltpu.SemaphoreType.DMA,
        ],
        compiler_params=pltpu.CompilerParams(vmem_limit_bytes=40 * 1024 * 1024),
        name="terms",
    )(data, pairs_t, groups_t))
    ring = range(n_pair)
    for k in sorted(ring, key=lambda k: -min(k, n_pair - k)):
        if k:
            parts[k] = lax.ppermute(parts[k], "pair", [(i, (i + k) % n_pair) for i in ring])
    return pl.pallas_call(
        place_kernel,
        out_shape=(
            jax.ShapeDtypeStruct((n_epochs // n_pair, tiles_dev, 2, LANES), jnp.float32),
            jax.ShapeDtypeStruct((n_pairs // 2, tiles_dev, LANES), jnp.float32),
        ),
        in_specs=[vector] * n_pair,
        out_specs=(vector, vector),
        compiler_params=pltpu.CompilerParams(vmem_limit_bytes=8 * 1024 * 1024),
        name="place",
    )(*parts)


def solution(mesh):
    placed = (P("tile", None, None, None), P(), P(), P())
    return jax.shard_map(
        local,
        mesh=mesh,
        in_specs=placed,
        out_specs=(P("pair", "tile", None, None), P("pair", "tile", None)),
        check_vma=False,
    )
```

```python
import functools

import jax
import jax.numpy as jnp
from jax import lax
from jax.experimental import pallas as pl
from jax.experimental.pallas import tpu as pltpu
from jax.sharding import PartitionSpec as P

EPS = 1e-06
LOOK_PIXELS = 64
LANES = 128
BATCH = 8


def split_dot(ones, x):
    high = x.astype(jnp.bfloat16)
    rest = x - high.astype(jnp.float32)
    middle = rest.astype(jnp.bfloat16)
    low = (rest - middle.astype(jnp.float32)).astype(jnp.bfloat16)
    width = x.shape[1]
    out = jnp.dot(ones, jnp.concatenate([high, middle, low], axis=1), preferred_element_type=jnp.float32)
    return out[:, :width] + out[:, width : 2 * width] + out[:, 2 * width :]


def across(x, lanes):
    return jnp.take_along_axis(x, lanes, axis=x.ndim - 1, mode="promise_in_bounds")


def order_kernel(source_ref, slc_ref, held, in_sem):
    n_dev, _, tiles_dev, _, part = held.shape
    n_chunks = in_sem.shape[0]
    chunk = n_dev // n_chunks
    start = pl.multiple_of(lax.axis_index("pair") * part, part)

    for c in range(n_chunks):

        @pl.loop(c * chunk, (c + 1) * chunk, unroll=4)
        def _(d):
            for k in range(tiles_dev):
                src = source_ref[d * tiles_dev + k]
                pltpu.make_async_copy(
                    slc_ref.at[:, src, :, pl.ds(start, part)], held.at[d, :, k], in_sem.at[c]
                ).start()

    for c in range(n_chunks):
        at = pl.ds(c * chunk, chunk)
        pltpu.make_async_copy(held.at[at], held.at[at], in_sem.at[c]).wait()


def terms_kernel(data_ref, pairs_ref, groups_ref, *refs):
    out_refs, (wide, norm, gamma, chosen_ref, rhs_ref, pairs_sm, sem) = refs[:-7], refs[-7:]
    pairs_copy = pltpu.make_async_copy(pairs_ref, pairs_sm, sem)
    pairs_copy.start()
    n_epochs = data_ref.shape[0]
    n_pairs = pairs_ref.shape[1]
    step = wide.shape[0]
    sub = lax.broadcasted_iota(jnp.int32, (8, LANES), 0)
    lane = lax.broadcasted_iota(jnp.int32, (8, LANES), 1)
    first = sub < 4
    rows_i = lax.broadcasted_iota(jnp.int32, (2 * LANES, LANES), 0)
    cols_i = lax.broadcasted_iota(jnp.int32, (2 * LANES, LANES), 1)
    same_look = ((rows_i % LANES) // 16 == cols_i // 16).astype(jnp.bfloat16)

    @pl.loop(0, n_epochs // step, unroll=8)
    def _(block):
        at = pl.ds(block * step, step)
        wide[...] = data_ref[at].astype(jnp.float32)
        re = wide[:, :, pl.ds(0, 16, stride=2), :]
        im = wide[:, :, pl.ds(1, 16, stride=2), :]
        power = re * re + im * im
        lines = power[:, :, 0:8] + power[:, :, 8:16]
        lines = jnp.where(first, lines[:, 0], lines[:, 1]) + pltpu.roll(
            jnp.where(first, lines[:, 1], lines[:, 0]), 4, 1
        )
        lines = lines.reshape(step * 8, LANES)
        high = lines.astype(jnp.bfloat16)
        low = (lines - high.astype(jnp.float32)).astype(jnp.bfloat16)
        level = jnp.dot(
            jnp.concatenate([high, low], axis=1), same_look, preferred_element_type=jnp.float32
        ).reshape(step, 8, LANES)
        inv = lax.rsqrt(level * (1.0 / LOOK_PIXELS) + EPS) * 0.125
        swapped = pltpu.roll(inv, 4, 1)
        for k, inv_k in enumerate((jnp.where(first, inv, swapped), jnp.where(first, swapped, inv))):
            inv_k = jnp.concatenate([inv_k, inv_k], axis=1)
            norm[at, 0, k] = re[:, k] * inv_k
            norm[at, 1, k] = im[:, k] * inv_k

    pairs_copy.wait()

    @pl.loop(0, n_pairs // BATCH, unroll=8)
    def _(batch):
        def one(j):
            q = batch * BATCH + j
            r = pairs_sm[0, q]
            t = pairs_sm[1, q]
            a_re, a_im = norm[r, 0], norm[r, 1]
            b_re, b_im = norm[t, 0], norm[t, 1]
            parts = []
            for cross in (a_re * b_re + a_im * b_im, a_im * b_re - a_re * b_im):
                s0 = cross[0, 0:8] + cross[0, 8:16]
                s1 = cross[1, 0:8] + cross[1, 8:16]
                parts.append(jnp.where(first, s0, s1) + pltpu.roll(jnp.where(first, s1, s0), 4, 0))
            return merge(parts[0], parts[1], 8)

        def merge(a, b, k):
            own = (lane & k) == 0
            return jnp.where(own, a, b) + across(jnp.where(own, b, a), lane ^ k)

        def tree(js, k):
            if len(js) == 1:
                return one(js[0])
            return merge(tree([j for j in js if not j & k], k // 2), tree([j for j in js if j & k], k // 2), k)

        z = tree(list(range(BATCH)), 4)
        gamma[batch] = z

    z = gamma[...]
    sub = lax.broadcasted_iota(jnp.int32, z.shape, 1)
    lane = lax.broadcasted_iota(jnp.int32, z.shape, 2)
    for k in (4, 2, 1):
        low_row = (sub & k) == 0
        moved = across(z.reshape(n_pairs, LANES), (lane ^ k).reshape(n_pairs, LANES)).reshape(z.shape)
        up, down = pltpu.roll(moved, 8 - k, 1), pltpu.roll(moved, k, 1)
        z = jnp.where(low_row == ((lane & k) == 0), z, jnp.where(low_row, up, down))
    z = z.reshape(n_pairs, LANES)
    comp0 = (lax.broadcasted_iota(jnp.int32, z.shape, 1) & 8) == 0
    square = z * z
    weight = square + jnp.where(comp0, pltpu.roll(square, LANES - 8, 1), pltpu.roll(square, 8, 1))
    refs, secs = pairs_ref[0:1, :], pairs_ref[1:2, :]
    epochs = lax.broadcasted_iota(jnp.int32, (n_epochs, n_pairs), 0)
    incidence = (epochs == secs).astype(jnp.float32) - (epochs == refs).astype(jnp.float32)
    rhs_ref[...] = split_dot(incidence.astype(jnp.bfloat16), weight * z)
    groups = groups_ref[0:1, :]
    mine = (lax.broadcasted_iota(jnp.int32, (8, n_pairs), 0) == groups).astype(jnp.float32)
    before = (
        lax.broadcasted_iota(jnp.int32, (n_pairs, n_pairs), 0)
        < lax.broadcasted_iota(jnp.int32, (n_pairs, n_pairs), 1)
    )
    ranks = jnp.dot(
        mine.astype(jnp.bfloat16), before.astype(jnp.bfloat16), preferred_element_type=jnp.float32
    )
    rank = jnp.sum(mine * ranks, axis=0, keepdims=True).astype(jnp.int32)
    half = n_pairs // 4
    slot = jnp.where(rank < half, groups * half + rank, n_pairs + groups * half + rank - half)
    hit = (lax.broadcasted_iota(jnp.int32, (2 * n_pairs, n_pairs), 0) == slot).astype(jnp.bfloat16)
    high = weight.astype(jnp.bfloat16).astype(jnp.float32)
    middle = (weight - high).astype(jnp.bfloat16).astype(jnp.float32)
    three = jnp.concatenate([jnp.where(comp0, high, middle), (weight - high) - middle], axis=1)
    chosen = jnp.dot(hit, three.astype(jnp.bfloat16), preferred_element_type=jnp.float32)
    first_half = chosen[:n_pairs, :LANES] + pltpu.roll(chosen[:n_pairs, :LANES], LANES - 8, 1)
    last_half = chosen[n_pairs:, :LANES] + pltpu.roll(chosen[n_pairs:, :LANES], 8, 1)
    chosen_ref[...] = jnp.where(
        comp0, first_half + chosen[:n_pairs, LANES:], last_half + chosen[n_pairs:, LANES:]
    )
    n_members = len(out_refs)
    half, e_out = n_pairs // n_members, n_epochs // n_members
    me = lax.axis_index("pair")
    for k, out_ref in enumerate(out_refs):
        to = lax.rem(me + k, n_members)
        out_ref[0:half, :] = chosen_ref[pl.ds(pl.multiple_of(to * half, half), half), :]
        out_ref[half : half + e_out, :] = rhs_ref[pl.ds(pl.multiple_of(to * e_out, e_out), e_out), :]


def place_kernel(*refs):
    part_refs, (rhs_ref, coherence_ref) = refs[:-2], refs[-2:]
    n_members = len(part_refs)
    rows = part_refs[0].shape[0]
    half = coherence_ref.shape[0] // 2
    width = LANES // n_members
    me = lax.axis_index("pair")
    lane = lax.broadcasted_iota(jnp.int32, (rows, LANES), 1)
    look = lane % width
    source = (look % 8) * 16 + look // 8
    owner = lane // width
    total = [None] * 4
    for k, part_ref in enumerate(part_refs):
        own = owner == lax.rem(me + n_members - k, n_members)
        part = part_ref[...]
        for g in range(4):
            piece = across(part, source + 4 * g)
            total[g] = piece if k == 0 else jnp.where(own, piece, total[g])
    for comp in range(2):
        for slot in range(2):
            coherence_ref[pl.ds(comp * half, half), slot, :] = total[comp * 2 + slot][:half]
            rhs_ref[:, slot, comp, :] = total[comp * 2 + slot][half:]


def local(slc, pairs, groups, tile_source):
    n_tile, n_pair = lax.axis_size("tile"), lax.axis_size("pair")
    e_dev, n_tiles, _, pixels = slc.shape
    tiles_dev = n_tiles // n_tile
    part = pixels // n_pair
    n_pairs = pairs.shape[0]
    n_epochs = e_dev * n_tile
    in_hbm = pl.BlockSpec(memory_space=pltpu.HBM)
    scalars = pl.BlockSpec(memory_space=pltpu.SMEM)
    vector = pl.BlockSpec(memory_space=pltpu.VMEM)
    pairs_t, groups_t = pairs.T, groups.reshape(1, n_pairs)
    out_shape = (n_tile, e_dev, tiles_dev, 2, part)
    chunks = 4
    ordered = pl.pallas_call(
        order_kernel,
        out_shape=jax.ShapeDtypeStruct(out_shape, slc.dtype),
        in_specs=[scalars, in_hbm],
        out_specs=vector,
        scratch_shapes=[
            pltpu.SemaphoreType.DMA((chunks,)),
        ],
        compiler_params=pltpu.CompilerParams(vmem_limit_bytes=48 * 1024 * 1024),
        name="order",
    )(tile_source, slc)
    data = lax.all_to_all(ordered, "tile", split_axis=0, concat_axis=0, tiled=True)
    data = data.reshape(n_epochs, tiles_dev, 2, part // LANES, LANES)
    data = jnp.swapaxes(data, 2, 3).reshape(n_epochs, tiles_dev, 2 * part // LANES, LANES)
    rows = n_pairs // 4 + n_epochs // n_pair
    parts = list(pl.pallas_call(
        terms_kernel,
        out_shape=[jax.ShapeDtypeStruct((rows, LANES), jnp.float32)] * n_pair,
        in_specs=[vector, vector, vector],
        out_specs=[vector] * n_pair,
        scratch_shapes=[
            pltpu.VMEM((16, tiles_dev, 32, LANES), jnp.float32),
            pltpu.VMEM((n_epochs, 2, tiles_dev, 16, LANES), jnp.float32),
            pltpu.VMEM((n_pairs // BATCH, BATCH, LANES), jnp.float32),
            pltpu.VMEM((n_pairs, LANES), jnp.float32),
            pltpu.VMEM((n_epochs, LANES), jnp.float32),
            pltpu.SMEM(pairs_t.shape, jnp.int32),
            pltpu.SemaphoreType.DMA,
        ],
        compiler_params=pltpu.CompilerParams(vmem_limit_bytes=40 * 1024 * 1024),
        name="terms",
    )(data, pairs_t, groups_t))
    ring = range(n_pair)
    for k in sorted(ring, key=lambda k: -min(k, n_pair - k)):
        if k:
            parts[k] = lax.ppermute(parts[k], "pair", [(i, (i + k) % n_pair) for i in ring])
    return pl.pallas_call(
        place_kernel,
        out_shape=(
            jax.ShapeDtypeStruct((n_epochs // n_pair, tiles_dev, 2, LANES), jnp.float32),
            jax.ShapeDtypeStruct((n_pairs // 2, tiles_dev, LANES), jnp.float32),
        ),
        in_specs=[vector] * n_pair,
        out_specs=(vector, vector),
        compiler_params=pltpu.CompilerParams(vmem_limit_bytes=8 * 1024 * 1024),
        name="place",
    )(*parts)


def solution(mesh):
    placed = (P("tile", None, None, None), P(), P(), P())
    return jax.shard_map(
        local,
        mesh=mesh,
        in_specs=placed,
        out_specs=(P("pair", "tile", None, None), P("pair", "tile", None)),
        check_vma=False,
    )
```
